32 devices in a mesh: dp: 4 (over z), seq: 4 (over y, x), head: 2 (over core).
Axes of the slice: x: 2, y: 2, z: 4, core: 2. Of those that a mesh axis runs over, the one named last changes fastest.
Arguments:
- block_input: bfloat16 [4, 1024, 1536], P('dp', 'seq'), may hold values from -6 to 6
- input_gain: float32 [1536], replicated, may hold values from 0.5 to 1.5
- gate_weight: bfloat16 [1536, 3072], P(None, 'head'), may hold values from -0.15625 to 0.15625
- inner_weight: bfloat16 [1536, 3072], P(None, 'head'), may hold values from -0.15625 to 0.15625
- state_weight: bfloat16 [1536, 256], replicated, may hold values from -0.15625 to 0.15625
- step_weight: bfloat16 [1536, 48], P(None, 'head'), may hold values from -0.15625 to 0.15625
- inner_filter: float32 [4, 3072], P(None, 'head'), may hold values from -3 to 3
- inner_filter_bias: float32 [3072], P('head'), may hold values from -3 to 3
- state_filter: float32 [4, 256], replicated, may hold values from -3 to 3
- state_filter_bias: float32 [256], replicated, may hold values from -3 to 3
- step_bias: float32 [48], P('head'), may hold values from -4 to -1
- decay_exponent: float32 [48], P('head'), may hold values from -10 to 0, as said below
- bypass_gain: float32 [48], P('head'), may hold values from 0.5 to 1.5
- mixer_gain: float32 [3072], P('head'), may hold values from 0.5 to 1.5
- output_weight: bfloat16 [3072, 1536], P('head'), may hold values from -0.109375 to 0.109375
- cotangent: bfloat16 [4, 1024, 1536], P('dp', 'seq'), may hold values from -6 to 6
Outputs:
- block_output: bfloat16 [4, 1024, 1536], P('dp', 'seq')
- input_gradient: float32 [4, 1024, 1536], P('dp', 'seq')
- input_gain_gradient: float32 [1536], P('head')
- gate_weight_gradient: float32 [1536, 3072], P(('dp', 'seq'), 'head')
- inner_weight_gradient: float32 [1536, 3072], P(('dp', 'seq'), 'head')
- state_weight_gradient: float32 [1536, 256], P(('dp', 'seq'))
- step_weight_gradient: float32 [1536, 48], P(('dp', 'seq'), 'head')
- inner_filter_gradient: float32 [4, 3072], P(None, 'head')
- inner_filter_bias_gradient: float32 [3072], P('head')
- state_filter_gradient: float32 [4, 256], replicated
- state_filter_bias_gradient: float32 [256], replicated
- step_bias_gradient: float32 [48], P('head')
- decay_exponent_gradient: float32 [48], P('head')
- bypass_gain_gradient: float32 [48], P('head')
- mixer_gain_gradient: float32 [3072], P('head')
- output_weight_gradient: float32 [3072, 1536], P('head', ('dp', 'seq'))
The draws below stay inside these ranges and needn't reach their ends.
Inputs may be any that keep to these rules, and one draw needn't show every extreme that they name: decay_exponent is the natural logarithm of each head's decay rate.
All inputs are finite; a program needn't handle non-finite values.
Results may differ from the reference program's by a relative error of at most 0.00155.
The reference program's roundings to bfloat16 on the way count: a program that leaves them out, or rounds other values in their place, can miss the bound.
Values may be sent and summed in bfloat16 or wider, within the bound.
No kernel may reach another device: no remote copies, remote signals or barrier semaphores. Data moves between devices by JAX's collectives and lax.ppermute only.
A program may use at most 128 MiB of HBM per device.

```python
import jax
import jax.numpy as jnp
from jax import lax

D = 1536
INNER = 3072
HEADS = 48
HEADDIM = 64
STATE = 128
CONV = 4
GROUP = 256
SEQ_LEN = 1024
SEQS = 4


def draw_decay_exponent(key, part):
    key = jax.random.fold_in(key, 7)
    lowest = jnp.log(0.5 / SEQ_LEN)
    return jax.random.uniform(key, (HEADS,), jnp.float32, lowest, 0.0)


def steps_of(own_key, extent, shards, least, high):
    def one(axis_at, shards_of):
        draws = jax.random.uniform(jax.random.fold_in(jax.random.fold_in(own_key, 6), axis_at), (shards_of,), jnp.float32, least / len(shards), high / len(shards))
        return jnp.repeat(jnp.exp(draws), extent[axis_at] // shards_of).reshape((-1,) + (1,) * (len(extent) - axis_at - 1))

    gain = one(*shards[0])
    for cut in shards[1:]:
        gain = gain * one(*cut)
    return gain


def bell_draw(own_key, extent, spread, reach, split=(), held_as=jnp.bfloat16):
    array = spread * jax.random.normal(own_key, extent, jnp.float32)
    if split:
        array = array * steps_of(own_key, extent, split, -0.22, 0.18)
    return jnp.clip(array, -reach, reach).astype(held_as)


def setup_inputs(seed: int = 0) -> dict:
    arg_keys = jax.random.split(jax.random.key(seed), 17)
    block_input = bell_draw(arg_keys[0], (SEQS, SEQ_LEN, D), 1.0, 6.0, ((0, 4), (1, 4)))
    input_gain = jnp.clip(1.0 + 0.1 * jax.random.normal(arg_keys[1], (D,), jnp.float32), 0.5, 1.5)
    gate_weight = bell_draw(arg_keys[2], (D, INNER), D ** -0.5, 0.15625, ((1, 2),))
    inner_weight = bell_draw(arg_keys[3], (D, INNER), D ** -0.5, 0.15625, ((1, 2),))
    state_weight = bell_draw(arg_keys[4], (D, 2 * STATE), D ** -0.5, 0.15625)
    step_weight = bell_draw(arg_keys[5], (D, HEADS), D ** -0.5, 0.15625, ((1, 2),))
    inner_filter = bell_draw(arg_keys[6], (CONV, INNER), CONV ** -0.5, 3.0, ((1, 2),), jnp.float32)
    inner_filter_bias = bell_draw(arg_keys[7], (INNER,), 0.5, 3.0, ((0, 2),), jnp.float32)
    state_filter = bell_draw(arg_keys[8], (CONV, 2 * STATE), CONV ** -0.5, 3.0, (), jnp.float32)
    state_filter_bias = bell_draw(arg_keys[9], (2 * STATE,), 0.5, 3.0, (), jnp.float32)
    step_bias = jnp.clip(-4.0 + 3.0 * jax.random.uniform(arg_keys[10], (HEADS,), jnp.float32) ** steps_of(arg_keys[10], (HEADS,), ((0, 2),), -0.2, 0.2), -4.0, -1.0)
    decay_exponent = draw_decay_exponent(jax.random.fold_in(arg_keys[16], 71), 0)
    bypass_gain = jnp.clip(0.5 + 1.0 * jax.random.uniform(arg_keys[12], (HEADS,), jnp.float32) ** steps_of(arg_keys[12], (HEADS,), ((0, 2),), -0.2, 0.2), 0.5, 1.5)
    mixer_gain = jnp.clip(1.0 + 0.1 * jax.random.normal(arg_keys[13], (INNER,), jnp.float32), 0.5, 1.5)
    output_weight = bell_draw(arg_keys[14], (INNER, D), INNER ** -0.5, 0.109375, ((0, 2),))
    cotangent = bell_draw(arg_keys[15], (SEQS, SEQ_LEN, D), 1.0, 6.0, ((0, 4), (1, 4)))
    return dict(block_input=block_input, input_gain=input_gain, gate_weight=gate_weight, inner_weight=inner_weight, state_weight=state_weight, step_weight=step_weight, inner_filter=inner_filter, inner_filter_bias=inner_filter_bias, state_filter=state_filter, state_filter_bias=state_filter_bias, step_bias=step_bias, decay_exponent=decay_exponent, bypass_gain=bypass_gain, mixer_gain=mixer_gain, output_weight=output_weight, cotangent=cotangent)


EPSILON = 1e-05
PRECISE = lax.Precision.HIGHEST

@jax.custom_vjp
def low(v):
    return lax.optimization_barrier(v.astype(jnp.bfloat16)).astype(jnp.float32)

@jax.custom_vjp
def low_back(v):
    return v

def low_keep(v):
    return (low(v), None)

def low_pass(kept, grad):
    return (grad,)

def back_keep(v):
    return (v, None)

def back_low(kept, grad):
    return (low(grad),)
low.defvjp(low_keep, low_pass)
low_back.defvjp(back_keep, back_low)

def matmul(first_operand, second_operand):
    return jnp.dot(first_operand, second_operand, precision=PRECISE)

def causal_conv(values, filters, offsets):
    length = values.shape[0]
    padding = jnp.zeros((filters.shape[0] - 1, values.shape[1]), jnp.float32)
    joined = jnp.concatenate([padding, values], axis=0)
    summed = offsets + filters[0] * joined[0:length]
    for position in range(1, filters.shape[0]):
        summed = summed + filters[position] * joined[position:position + length]
    return jax.nn.silu(summed)

def block_step(carry_state, pieces):
    head_rows, step_size, decay_rows, input_part, output_part = pieces
    cumulative = jnp.cumsum(decay_rows, axis=0)
    span_rows = cumulative.shape[0]
    causal = (jnp.arange(span_rows)[:, None] >= jnp.arange(span_rows)[None, :])[:, :, None]
    differ = cumulative[:, None, :] - cumulative[None, :, :]
    factor = jnp.where(causal, jnp.exp(jnp.where(causal, differ, 0.0)), 0.0)
    scores = jnp.dot(output_part, input_part.T, precision=PRECISE)
    mixing = scores[:, :, None] * factor * step_size[None, :, :]
    within = jnp.einsum('ijh,jhp->ihp', mixing, head_rows, precision=PRECISE)
    carried = jnp.einsum('in,hpn->ihp', output_part, carry_state, precision=PRECISE) * jnp.exp(cumulative)[:, :, None]
    tail_weight = jnp.exp(cumulative[-1:] - cumulative) * step_size
    fresh_state = jnp.einsum('jh,jhp,jn->hpn', tail_weight, head_rows, input_part, precision=PRECISE)
    carry_state = jnp.exp(cumulative[-1])[:, None, None] * carry_state + fresh_state
    return (carry_state, within + carried)

def sequence_mixer(head_rows, step_size, decay_rows, input_rows, output_rows):
    length = head_rows.shape[0]

    def blocks(tensor):
        return tensor.reshape((length // GROUP, GROUP) + tensor.shape[1:])
    initial = jnp.zeros((head_rows.shape[1], head_rows.shape[2], input_rows.shape[1]), jnp.float32)
    final_state, outputs = lax.scan(jax.checkpoint(block_step), initial, (blocks(head_rows), blocks(step_size), blocks(decay_rows), blocks(input_rows), blocks(output_rows)))
    return outputs.reshape(head_rows.shape)

def block_forward(params, tokens):
    input_gain, gate_weight, inner_weight, state_weight, step_weight, inner_filter, inner_filter_bias, state_filter, state_filter_bias, step_bias, decay_exponent, bypass_gain, mixer_gain, output_weight = params
    length = tokens.shape[0]
    inverse = lax.rsqrt(lax.optimization_barrier(jnp.mean(tokens * tokens, axis=1, keepdims=True)) + EPSILON)
    normed = low(tokens * inverse * input_gain)
    gate_rows = low_back(matmul(normed, gate_weight))
    inner_rows = low_back(matmul(normed, inner_weight))
    state_rows = low_back(matmul(normed, state_weight))
    step_input = low_back(matmul(normed, step_weight))
    conv_inner = causal_conv(inner_rows, inner_filter, inner_filter_bias)
    conv_state = causal_conv(state_rows, state_filter, state_filter_bias)
    step_size = jax.nn.softplus(step_input + step_bias)
    decay_rows = -jnp.exp(decay_exponent) * step_size
    head_rows = conv_inner.reshape(length, HEADS, HEADDIM)
    mixed = sequence_mixer(head_rows, step_size, decay_rows, conv_state[:, :STATE], conv_state[:, STATE:])
    mixed = (mixed + bypass_gain[:, None] * head_rows).reshape(length, INNER)
    gated = mixed * jax.nn.silu(gate_rows)
    scale = lax.rsqrt(lax.optimization_barrier(jnp.mean(gated * gated, axis=1, keepdims=True)) + EPSILON)
    normed_out = low(gated * scale * mixer_gain)
    return tokens + matmul(normed_out, output_weight)

def reference(block_input, input_gain, gate_weight, inner_weight, state_weight, step_weight, inner_filter, inner_filter_bias, state_filter, state_filter_bias, step_bias, decay_exponent, bypass_gain, mixer_gain, output_weight, cotangent):
    params = tuple((weight.astype(jnp.float32) for weight in (input_gain, gate_weight, inner_weight, state_weight, step_weight, inner_filter, inner_filter_bias, state_filter, state_filter_bias, step_bias, decay_exponent, bypass_gain, mixer_gain, output_weight)))

    def one_sequence(totals, sequence_pair):
        tokens, back_rows = sequence_pair
        result, pullback = jax.vjp(block_forward, params, tokens)
        param_grads, token_grads = pullback(back_rows)
        return (jax.tree.map(jnp.add, totals, param_grads), (result.astype(jnp.bfloat16), token_grads))
    initial = jax.tree.map(jnp.zeros_like, params)
    totals, (block_output, input_gradient) = lax.scan(one_sequence, initial, (block_input.astype(jnp.float32), cotangent.astype(jnp.float32)))
    return (block_output, input_gradient, totals[0], totals[1], totals[2], totals[3], totals[4], totals[5], totals[6], totals[7], totals[8], totals[9], totals[10], totals[11], totals[12], totals[13])
```

```python
import jax
import jax.numpy as jnp
from jax import lax
from jax.sharding import PartitionSpec as P

D = 1536
INNER = 3072
GROUP = 256


EPSILON = 1e-05
PRECISE = lax.Precision.HIGHEST

def swap(block, axis, distance):
    route = [(i, i ^ distance) for i in range(lax.axis_size(axis))]
    return lax.ppermute(block, axis, route)


def rotated(block, axis, distance):
    count = lax.axis_size(axis)
    return lax.ppermute(block, axis, [(i, (i + distance) % count) for i in range(count)])


def sum_all(block, axes):
    for axis in axes:
        distance = 1
        while distance < lax.axis_size(axis):
            block = block + swap(block, axis, distance)
            distance *= 2
    return block


def sum_heads(block):
    return sum_all(block, ("head",))


def seq_pieces(pieces):
    count = lax.axis_size("seq")
    place = lax.axis_index("seq")
    own = lax.dynamic_index_in_dim(pieces, place, 0, False)
    arrived = [
        rotated(lax.dynamic_index_in_dim(pieces, (place + k) % count, 0, False), "seq", k)
        for k in range(1, count)
    ]
    return jnp.concatenate([own] + arrived, axis=0)


def seq_gather(block):
    count = lax.axis_size("seq")
    return jnp.concatenate([block] + [rotated(block, "seq", k) for k in range(1, count)], axis=0)


def dp_reduce(partial):
    count = lax.axis_size("dp")
    place = lax.axis_index("dp")
    largest = jnp.maximum(jnp.max(jnp.abs(partial)), 1e-25)
    packed = (partial * (16384.0 / largest)).astype(jnp.float16)
    unit = jnp.full((8, 128), largest / 16384.0, jnp.float32)
    total = lax.dynamic_index_in_dim(partial, place, 0, False)
    for k in range(1, count):
        piece = lax.dynamic_index_in_dim(packed, (place + k) % count, 0, False)
        total = total + rotated(piece, "dp", k).astype(jnp.float32) * rotated(unit, "dp", k)[0, 0]
    return total


def running_sum(values, axis):
    length = values.shape[axis]
    order = (
        lax.broadcasted_iota(jnp.int32, (length, length), 0)
        <= lax.broadcasted_iota(jnp.int32, (length, length), 1)
    ).astype(jnp.float32)
    moved = jnp.moveaxis(values, axis, -1)
    return jnp.moveaxis(jnp.einsum("...j,ji->...i", moved, order, precision=PRECISE), -1, axis)


def shifted(block, axis, distance):
    devices = range(lax.axis_size(axis))
    route = [(i - distance, i) for i in devices if i - distance in devices]
    return lax.ppermute(block, axis, route)


def carried_in(part, axis, combine, identity, reverse):
    count = lax.axis_size(axis)
    place = lax.axis_index(axis)
    ahead = count - 1 - place if reverse else place
    gathered = jax.tree.map(lambda a: lax.all_gather(a, axis), part)
    state = jax.tree.map(lambda a, e: jnp.zeros_like(a) + jnp.asarray(e, a.dtype), part, identity)

    def one(lap, state):
        source = count - 1 - lap if reverse else lap
        return combine(
            state, jax.tree.map(lambda a: lax.dynamic_index_in_dim(a, source, 0, False), gathered)
        )

    return lax.fori_loop(0, ahead, one, state)


def project(activations, weights):
    return jnp.einsum("std,dc->stc", activations, weights, preferred_element_type=jnp.float32)


def project_back(gradients, weights):
    return jnp.einsum("stc,dc->std", gradients, weights, preferred_element_type=jnp.float32)


def weight_gradient(activations, gradients):
    return jnp.einsum("std,stc->dc", activations, gradients, preferred_element_type=jnp.float32)


def conv_silu(tail_rows, values, filters, offsets):
    length = values.shape[1]
    joined = jnp.concatenate([tail_rows, values], axis=1)
    summed = offsets + filters[0] * joined[:, 0:length]
    for position in range(1, filters.shape[0]):
        summed = summed + filters[position] * joined[:, position : position + length]
    return jax.nn.silu(summed)


def split_blocks(tensor, dimension, block_size):
    dims_before = tensor.shape
    reshaped = tensor.reshape(
        dims_before[:dimension]
        + (dims_before[dimension] // block_size, block_size)
        + dims_before[dimension + 1 :]
    )
    return jnp.moveaxis(reshaped, dimension, 0)


def block_step(carry_state, pieces):
    head_rows, step_size, decay_rows, input_part, output_part = pieces
    cumulative = running_sum(decay_rows, 2)
    span_rows = cumulative.shape[2]
    causal = lax.broadcasted_iota(jnp.int32, (span_rows, span_rows), 0) >= lax.broadcasted_iota(
        jnp.int32, (span_rows, span_rows), 1
    )
    differ = cumulative[:, :, :, None] - cumulative[:, :, None, :]
    factor = jnp.where(causal, jnp.exp(jnp.where(causal, differ, 0.0)), 0.0)
    scores = jnp.einsum("sin,sjn->sij", output_part, input_part, precision=PRECISE)
    mixing = scores[:, None] * factor * step_size[:, :, None, :]
    within = jnp.einsum("shij,sjhp->sihp", mixing, head_rows, precision=PRECISE)
    carried = (
        jnp.einsum("sin,shpn->sihp", output_part, carry_state, precision=PRECISE)
        * jnp.exp(jnp.swapaxes(cumulative, 1, 2))[..., None]
    )
    tail_weight = jnp.exp(cumulative[:, :, -1:] - cumulative) * step_size
    fresh_state = jnp.einsum(
        "shj,sjhp,sjn->shpn", tail_weight, head_rows, input_part, precision=PRECISE
    )
    carry_state = jnp.exp(cumulative[:, :, -1])[..., None, None] * carry_state + fresh_state
    return (carry_state, within + carried)


def device_mixer(
    inner_rows,
    conv_state,
    step_input,
    tail_inner,
    inner_filter,
    inner_filter_bias,
    step_bias,
    decay_exponent,
    bypass_gain,
):
    inner_width = inner_rows.shape[2]
    state_width = conv_state.shape[2] // 2
    conv_inner = conv_silu(tail_inner, inner_rows, inner_filter, inner_filter_bias)
    seq_count, length, head_count = step_input.shape
    head_width = inner_width // head_count
    step_size = jnp.swapaxes(jax.nn.softplus(step_input + step_bias), 1, 2)
    decay_rows = -jnp.exp(decay_exponent)[None, :, None] * step_size
    head_rows = conv_inner.reshape(seq_count, length, head_count, head_width)
    input_rows = conv_state[:, :, :state_width]
    output_rows = conv_state[:, :, state_width:]
    initial = jnp.zeros((seq_count, head_count, head_width, state_width), jnp.float32)
    end_state, outputs = lax.scan(
        jax.checkpoint(block_step),
        initial,
        (
            split_blocks(head_rows, 1, GROUP),
            split_blocks(step_size, 2, GROUP),
            split_blocks(decay_rows, 2, GROUP),
            split_blocks(input_rows, 1, GROUP),
            split_blocks(output_rows, 1, GROUP),
        ),
    )
    local_out = jnp.moveaxis(outputs, 0, 1).reshape(seq_count, length, head_count, head_width)
    local_out = local_out + bypass_gain[:, None] * head_rows
    cumdev = jnp.swapaxes(running_sum(decay_rows, 2), 1, 2)
    return (end_state, cumdev[:, -1], local_out, output_rows, cumdev)


def add_incoming(local_out, output_rows, cumdev, incoming):
    reach = jnp.einsum("stn,shpn->sthp", output_rows, incoming, precision=PRECISE)
    mixed = local_out + jnp.exp(cumdev)[..., None] * reach
    return mixed.reshape(mixed.shape[0], mixed.shape[1], -1)


def chain_pair(earlier, later):
    decay_early, state_early = earlier
    decay_later, state_later = later
    return (decay_early * decay_later, decay_later[..., None, None] * state_early + state_later)


def per_device(
    block_input,
    input_gain,
    gate_weight,
    inner_weight,
    state_weight,
    step_weight,
    inner_filter,
    inner_filter_bias,
    state_filter,
    state_filter_bias,
    step_bias,
    decay_exponent,
    bypass_gain,
    mixer_gain,
    output_weight,
    cotangent,
):
    residual = block_input.astype(jnp.float32)
    inverse = lax.rsqrt(jnp.mean(residual * residual, axis=2, keepdims=True) + EPSILON)
    normed = (residual * inverse * input_gain).astype(jnp.bfloat16)
    gate_rows = project(normed, gate_weight)
    inner_rows = project(normed, inner_weight)
    state_rows = project(normed, state_weight)
    step_input = project(normed, step_weight)
    inner_width = inner_rows.shape[2]
    edge_rows = inner_filter.shape[0] - 1
    ending = jnp.concatenate([inner_rows[:, -edge_rows:], state_rows[:, -edge_rows:]], axis=2)
    tail_rows = shifted(ending, "seq", 1)
    conv_state, state_conv_back = jax.vjp(
        conv_silu, tail_rows[:, :, inner_width:], state_rows, state_filter, state_filter_bias
    )
    outputs, mixer_back = jax.vjp(
        device_mixer,
        inner_rows,
        conv_state,
        step_input,
        tail_rows[:, :, :inner_width],
        inner_filter,
        inner_filter_bias,
        step_bias,
        decay_exponent,
        bypass_gain,
    )
    end_state, log_total, local_out, output_rows, cumdev = outputs
    decay_total = jnp.exp(log_total)
    incoming = carried_in(
        (decay_total, end_state),
        "seq",
        chain_pair,
        (jnp.ones_like(decay_total), jnp.zeros_like(end_state)),
        False,
    )[1]
    mixed, incoming_back = jax.vjp(add_incoming, local_out, output_rows, cumdev, incoming)
    sigma = jax.nn.sigmoid(gate_rows)
    gated = mixed * (gate_rows * sigma)
    total_squares = sum_heads(jnp.sum(gated * gated, axis=2))
    scale = lax.rsqrt(total_squares[..., None] / INNER + EPSILON)
    normed_out = (gated * scale * mixer_gain).astype(jnp.bfloat16)
    branch = lax.psum_scatter(
        project(normed_out, output_weight), "head", scatter_dimension=2, tiled=True
    )
    half_width = branch.shape[2]
    feature_start = lax.axis_index("head") * half_width
    residual_half = lax.dynamic_slice_in_dim(residual, feature_start, half_width, 2)
    output_half = (residual_half + branch).astype(jnp.bfloat16)
    block_output = lax.all_gather(output_half, "head", axis=2, tiled=True)
    output_weight_gradient = weight_gradient(normed_out, cotangent)
    normed_grad = project_back(cotangent, output_weight)
    mixer_gain_gradient = jnp.sum(normed_grad * gated * scale, axis=(0, 1))
    scaled_grad = normed_grad * mixer_gain
    inner_dot = sum_heads(jnp.sum(scaled_grad * gated, axis=2))
    gated_grad = scale * scaled_grad - gated * (scale * scale * scale) * (
        inner_dot[..., None] / INNER
    )
    mixed_grad = gated_grad * gate_rows * sigma
    gate_grad = (gated_grad * mixed * sigma * (1.0 + gate_rows * (1.0 - sigma))).astype(
        jnp.bfloat16
    )
    local_grad, output_grad, cumdev_grad, incoming_grad = incoming_back(mixed_grad)
    later_grad = carried_in(
        (decay_total, incoming_grad),
        "seq",
        chain_pair,
        (jnp.ones_like(decay_total), jnp.zeros_like(incoming_grad)),
        True,
    )[1]
    decay_grad = jnp.sum(later_grad * incoming, axis=(2, 3)) * decay_total
    (
        inner_grad,
        conv_state_grad,
        step_grad,
        tail_inner_grad,
        inner_filter_gradient,
        inner_filter_bias_gradient,
        step_bias_gradient,
        decay_exponent_gradient,
        bypass_gain_gradient,
    ) = mixer_back((later_grad, decay_grad, local_grad, output_grad, cumdev_grad))
    conv_state_grad = sum_heads(conv_state_grad)
    tail_state_grad, state_grad, state_filter_gradient, state_filter_bias_gradient = (
        state_conv_back(conv_state_grad)
    )
    tail_grad = jnp.concatenate([tail_inner_grad, tail_state_grad], axis=2)
    arrived = shifted(tail_grad, "seq", -1)
    inner_grad = jnp.concatenate(
        [inner_grad[:, :-edge_rows], inner_grad[:, -edge_rows:] + arrived[:, :, :inner_width]],
        axis=1,
    )
    state_grad = jnp.concatenate(
        [state_grad[:, :-edge_rows], state_grad[:, -edge_rows:] + arrived[:, :, inner_width:]],
        axis=1,
    )
    inner_rounded = inner_grad.astype(jnp.bfloat16)
    state_rounded = state_grad.astype(jnp.bfloat16)
    step_rounded = step_grad.astype(jnp.bfloat16)
    first_head = (lax.axis_index("head") == 0).astype(jnp.float32)
    normed_back = (
        project_back(gate_grad, gate_weight)
        + project_back(inner_rounded, inner_weight)
        + project_back(step_rounded, step_weight)
        + first_head * project_back(state_rounded, state_weight)
    )
    back_half = lax.psum_scatter(normed_back, "head", scatter_dimension=2, tiled=True)
    gain_half = lax.dynamic_slice_in_dim(input_gain, feature_start, half_width, 0)
    cot_half = lax.dynamic_slice_in_dim(cotangent, feature_start, half_width, 2).astype(jnp.float32)
    input_gain_gradient = jnp.sum(back_half * residual_half * inverse, axis=(0, 1))
    gain_back = back_half * gain_half
    input_dot = sum_heads(jnp.sum(gain_back * residual_half, axis=2))
    gradient_half = (
        gain_back * inverse
        - residual_half * (inverse * inverse * inverse) * (input_dot[..., None] / D)
        + cot_half
    )
    input_gradient = lax.all_gather(gradient_half, "head", axis=2, tiled=True)
    def split_columns(tokens):
        rows = tokens.reshape(-1, tokens.shape[-1])
        parts = rows.reshape(rows.shape[0], lax.axis_size("dp"), lax.axis_size("seq"), -1)
        pieces = jnp.moveaxis(parts, 2, 0)
        return seq_pieces(pieces.reshape(pieces.shape[0], rows.shape[0], -1))

    def summed(first, second):
        partial = jnp.einsum("tdw,tc->dwc", first, second, preferred_element_type=jnp.float32)
        return dp_reduce(partial)

    def summed_out(first, second):
        partial = jnp.einsum("tc,tdw->dcw", first, second, preferred_element_type=jnp.float32)
        return dp_reduce(partial)

    dp_count = lax.axis_size("dp")
    normed_pieces = split_columns(normed)
    normed_pieces = normed_pieces.reshape(normed_pieces.shape[0], dp_count, -1)
    cot_pieces = split_columns(cotangent)
    cot_pieces = cot_pieces.reshape(cot_pieces.shape[0], dp_count, -1)

    def rows_of(t):
        return t.reshape(-1, t.shape[-1])

    last = jnp.concatenate([rows_of(inner_rounded), rows_of(state_rounded), rows_of(step_rounded)], axis=1)
    last_sum = summed(normed_pieces, seq_gather(last))
    state_width = state_rounded.shape[2]
    row_sums = (
        summed(normed_pieces, seq_gather(rows_of(gate_grad))),
        last_sum[:, :inner_width],
        last_sum[:, inner_width : inner_width + state_width],
        last_sum[:, inner_width + state_width :],
        summed_out(seq_gather(rows_of(normed_out)), cot_pieces),
    )
    gain_whole = lax.all_gather(input_gain_gradient, "head", axis=0, tiled=True)
    parts = (
        gain_whole,
        mixer_gain_gradient,
        inner_filter_gradient,
        inner_filter_bias_gradient,
        state_filter_gradient,
        state_filter_bias_gradient,
        step_bias_gradient,
        decay_exponent_gradient,
        bypass_gain_gradient,
    )
    flat = jnp.concatenate([p.reshape(-1) for p in parts])
    width = flat.shape[0]
    flat = jnp.pad(flat, (0, -width % 1024)).reshape(8, -1)
    flat = sum_all(flat, ("seq", "dp")).reshape(-1)
    small = []
    start = 0
    for p in parts:
        small.append(flat[start : start + p.size].reshape(p.shape))
        start += p.size
    small[0] = lax.dynamic_slice_in_dim(small[0], feature_start, half_width, 0)
    return (
        block_output,
        input_gradient,
        small[0],
        row_sums[0],
        row_sums[1],
        row_sums[2],
        row_sums[3],
        small[2],
        small[3],
        small[4],
        small[5],
        small[6],
        small[7],
        small[8],
        small[1],
        row_sums[4],
    )


def solution(mesh):
    return jax.shard_map(
        per_device,
        mesh=mesh,
        in_specs=(
            P("dp", "seq", None),
            P(),
            P(None, "head"),
            P(None, "head"),
            P(),
            P(None, "head"),
            P(None, "head"),
            P("head"),
            P(),
            P(),
            P("head"),
            P("head"),
            P("head"),
            P("head"),
            P("head", None),
            P("dp", "seq", None),
        ),
        out_specs=(
            P("dp", "seq", None),
            P("dp", "seq", None),
            P("head"),
            P(("dp", "seq"), "head"),
            P(("dp", "seq"), "head"),
            P(("dp", "seq"), None),
            P(("dp", "seq"), "head"),
            P(None, "head"),
            P("head"),
            P(),
            P(),
            P("head"),
            P("head"),
            P("head"),
            P("head"),
            P("head", ("dp", "seq")),
        ),
        check_vma=False,
    )
```
